768 devices in a mesh: row: 8 (over y), col: 96 (over z, x, core).
Axes of the slice: x: 4, y: 8, z: 12, core: 2. Of those that a mesh axis runs over, the one named last changes fastest.
Arguments:
- image_mantissa: bfloat16 [6144, 1536], P(('row', 'col')), may hold values from -4 to 4
- image_exponent: int32 [6144], P(('row', 'col')), may hold values from -2 to 2
- text_mantissa: bfloat16 [6144, 1536], P(('col', 'row')), may hold values from -4 to 4
- text_exponent: int32 [6144], P(('col', 'row')), may hold values from -2 to 2
- positive: int32 [6144], P('row'), may hold values from 0 to 6143, each once
- logit_scale: float32 [1], replicated, may hold values from 4 to 16
- logit_bias: float32 [1], replicated, may hold values from -4 to -1
Outputs:
- image_grad: float32 [6144, 1536], P(('row', 'col'))
- text_grad: float32 [6144, 1536], P(('col', 'row'))
The draws below stay inside these ranges and needn't reach their ends.
Inputs may be any that keep to these rules, and one draw needn't show every extreme that they name: positive is a permutation of the 6144 text indices.
All inputs are finite; a program needn't handle non-finite values.
Results may differ from the reference program's by a relative error of at most 0.0041.
Values may be sent and summed in bfloat16 or wider, within the bound.
No kernel may reach another device: no remote copies, remote signals or barrier semaphores. Data moves between devices by JAX's collectives and lax.ppermute only.
A program may use at most 32 MiB of HBM per device.

```python
import math
import jax
import jax.numpy as jnp
from jax import lax

D = 1536
R = 8
B = 6144
N_ROW = 8
N_COL = 96


def with_ends(result, rng, least, top_value):
    spot = [jax.random.randint(jax.random.fold_in(rng, axis), (), 0, length) for axis, length in enumerate(result.shape)]
    widest = result.shape.index(max(result.shape))
    next_to = spot[:widest] + [(spot[widest] + 1) % result.shape[widest]] + spot[widest + 1:]
    return result.at[tuple(spot)].set(least).at[tuple(next_to)].set(top_value)


def level_of(stream_key, shape, shards, least, top_value):
    def one(dim, shards_of):
        heights = jax.random.uniform(jax.random.fold_in(jax.random.fold_in(stream_key, 6), dim), (shards_of,), jnp.float32, least / len(shards), top_value / len(shards))
        return jnp.repeat(jnp.exp(heights), shape[dim] // shards_of).reshape((-1,) + (1,) * (len(shape) - dim - 1))

    loudness = one(*shards[0])
    for cut in shards[1:]:
        loudness = loudness * one(*cut)
    return loudness


def scatter_about(rng, dims, spread, most, pieces=(), kind=jnp.bfloat16):
    level = level_of(rng, dims, pieces, -0.22, 0.18) if pieces else 1.0
    drawn = jax.random.normal(rng, dims, jnp.float32) * spread * level
    return jnp.minimum(jnp.maximum(drawn, -most), most).astype(kind)


def setup_inputs(seed: int = 0) -> dict:
    arg_keys = jax.random.split(jax.random.key(seed), 8)
    return {
        "image_mantissa": scatter_about(arg_keys[0], (B, D), 1.0, 4.0, ((0, 768),)),
        "image_exponent": with_ends(jax.random.randint(arg_keys[1], (B,), -2, 3), jax.random.fold_in(arg_keys[1], 1), -2, 2).astype(jnp.int32),
        "text_mantissa": scatter_about(arg_keys[2], (B, D), 1.0, 4.0, ((0, 768),)),
        "text_exponent": with_ends(jax.random.randint(arg_keys[3], (B,), -2, 3), jax.random.fold_in(arg_keys[3], 1), -2, 2).astype(jnp.int32),
        "positive": jax.random.permutation(arg_keys[4], B).astype(jnp.int32),
        "logit_scale": jnp.clip(jnp.exp(jax.random.uniform(arg_keys[5], (1,), jnp.float32, math.log(4.0), math.log(16.0))), 4.0, 16.0),
        "logit_bias": jnp.clip(jax.random.uniform(arg_keys[6], (1,), jnp.float32, -4.0, -1.0), -4.0, -1.0),
    }


epsilon = 1e-06

def unit_rows(mantissa, exponent):
    scaled = mantissa.astype(jnp.float32) * jnp.exp2(exponent.astype(jnp.float32))[:, None]
    norm = jnp.sqrt(lax.optimization_barrier(jnp.sum(scaled * scaled, axis=1, keepdims=True)) + epsilon)
    unit = scaled / norm
    return (norm, unit, unit.astype(jnp.bfloat16))

def reference(image_mantissa, image_exponent, text_mantissa, text_exponent, positive, logit_scale, logit_bias):
    image_norm, image_unit, image_half = unit_rows(image_mantissa, image_exponent)
    text_norm, text_unit, text_half = unit_rows(text_mantissa, text_exponent)
    factor = logit_scale[0]
    offset = logit_bias[0]
    block_rows = R * N_COL
    text_ids = jnp.arange(B, dtype=jnp.int32)

    def one_block(text_accum, inputs):
        image_block, pair_block = inputs
        logits = factor * jnp.dot(image_block, text_half.T, preferred_element_type=jnp.float32) + offset
        label_sign = jnp.where(pair_block[:, None] == text_ids[None, :], 1.0, -1.0).astype(jnp.float32)
        margin = label_sign * logits
        pair_half = (-label_sign * jax.nn.sigmoid(-margin)).astype(jnp.bfloat16)
        image_part = factor * jnp.dot(pair_half, text_half, preferred_element_type=jnp.float32)
        text_accum = text_accum + factor * jnp.dot(pair_half.T, image_block, preferred_element_type=jnp.float32)
        return (text_accum, image_part)
    blocks = (image_half.reshape(N_ROW, block_rows, D), positive.reshape(N_ROW, block_rows))
    text_accum, image_parts = lax.scan(one_block, jnp.zeros((B, D), jnp.float32), blocks)
    unit_grad_image = image_parts.reshape(B, D)
    image_grad = (unit_grad_image - image_unit * lax.optimization_barrier(jnp.sum(image_unit * unit_grad_image, axis=1, keepdims=True))) / image_norm
    text_grad = (text_accum - text_unit * lax.optimization_barrier(jnp.sum(text_unit * text_accum, axis=1, keepdims=True))) / text_norm
    return (image_grad, text_grad)
```

```python
import jax
import jax.numpy as jnp
from jax import lax
from jax.sharding import Mesh, PartitionSpec as P

epsilon = 1e-06
AXES = ("y", "z", "x", "core")
NY, NZ, NX, NC = 8, 12, 4, 2
R = 8
f32 = jnp.float32
bf16 = jnp.bfloat16


def unit_rows(mantissa, exponent):
    scaled = mantissa.astype(f32) * jnp.exp2(exponent.astype(f32))[:, None]
    norm = jnp.sqrt(jnp.sum(scaled * scaled, axis=1, keepdims=True) + epsilon)
    unit = scaled / norm
    return (norm, unit, unit.astype(bf16))


def exchange(blocks, axis):
    return lax.all_to_all(blocks, axis, split_axis=0, concat_axis=0, tiled=True)


def spread(block, axis, n):
    return exchange(jnp.broadcast_to(block[None], (n,) + block.shape), axis)


def tangent(unit_grad, unit, norm):
    return (unit_grad - unit * jnp.sum(unit * unit_grad, axis=1, keepdims=True)) / norm


def shards(
    image_mantissa, image_exponent, text_mantissa, text_exponent, positive, logit_scale, logit_bias
):
    d = image_mantissa.shape[1]
    image_norm, image_unit, image_half = unit_rows(image_mantissa, image_exponent)
    text_norm, text_unit, text_half = unit_rows(text_mantissa, text_exponent)
    factor = logit_scale[0]
    offset = logit_bias[0]
    z, x, c = lax.axis_index("z"), lax.axis_index("x"), lax.axis_index("core")

    images = spread(image_half, "z", NZ).reshape(NZ * R, d)
    images = lax.all_gather(images, "core", axis=0, tiled=True)
    texts = spread(text_half, "y", NY).reshape(NY * R, d)
    texts = lax.all_gather(texts, "x", axis=0, tiled=True)

    place = positive.reshape(NZ, NX, NC, R)
    place = lax.dynamic_index_in_dim(place, x, axis=1, keepdims=False)
    place = place.transpose(1, 0, 2).reshape(NC * NZ * R)
    xs = jnp.arange(NX, dtype=jnp.int32)[:, None]
    yr = jnp.arange(NY * R, dtype=jnp.int32)[None, :]
    text_ids = (((z * NX + xs) * NC + c) * (NY * R) + yr).reshape(NX * NY * R)

    logits = factor * jnp.dot(images, texts.T, preferred_element_type=f32) + offset
    label_sign = jnp.where(place[:, None] == text_ids[None, :], 1.0, -1.0).astype(f32)
    weights = (-label_sign * jax.nn.sigmoid(-label_sign * logits)).astype(bf16)

    part = factor * jnp.dot(weights, texts, preferred_element_type=f32)
    part = exchange(part.reshape(NC, NZ * R, d), "core").sum(axis=0).astype(bf16)
    part = exchange(part.reshape(NZ, R, d), "z")
    unit_grad_image = part.astype(f32).sum(axis=0)

    part = (factor * jnp.dot(weights.T, images, preferred_element_type=f32)).astype(bf16)
    part = exchange(part.reshape(NX, NY * R, d), "x").astype(f32).sum(axis=0).astype(bf16)
    part = exchange(part.reshape(NY, R, d), "y")
    unit_grad_text = part.astype(f32).sum(axis=0)

    return (
        tangent(unit_grad_image, image_unit, image_norm),
        tangent(unit_grad_text, text_unit, text_norm),
    )


def solution(mesh):
    fine = Mesh(mesh.devices.reshape(NY, NZ, NX, NC), AXES)
    image = ("y", "z", "x", "core")
    text = ("z", "x", "core", "y")
    return jax.shard_map(
        shards,
        mesh=fine,
        in_specs=(P(image, None), P(image), P(text, None), P(text), P("y"), P(), P()),
        out_specs=(P(image, None), P(text, None)),
        check_vma=False,
    )
```

```python
import jax
import jax.numpy as jnp
from jax import lax
from jax.sharding import Mesh, PartitionSpec as P

epsilon = 1e-06
AXES = ("y", "z", "x", "core")
NY, NZ, NX, NC = 8, 12, 4, 2
R = 8
f32 = jnp.float32
bf16 = jnp.bfloat16


def unit_rows(mantissa, exponent):
    scaled = mantissa.astype(f32) * jnp.exp2(exponent.astype(f32))[:, None]
    norm = jnp.sqrt(jnp.sum(scaled * scaled, axis=1, keepdims=True) + epsilon)
    unit = scaled / norm
    return (norm, unit, unit.astype(bf16))


def exchange(blocks, axis):
    return lax.all_to_all(blocks, axis, split_axis=0, concat_axis=0, tiled=True)


def spread(block, axis, n):
    return exchange(jnp.broadcast_to(block[None], (n,) + block.shape), axis)


def shift(block, axis, n, k):
    return lax.ppermute(block, axis, [(i, (i + k) % n) for i in range(n)])


def tangent(unit_grad, unit, norm):
    return (unit_grad - unit * jnp.sum(unit * unit_grad, axis=1, keepdims=True)) / norm


def shards(
    image_mantissa, image_exponent, text_mantissa, text_exponent, positive, logit_scale, logit_bias
):
    d = image_mantissa.shape[1]
    text_norm, text_unit, text_half = unit_rows(text_mantissa, text_exponent)
    image_norm, image_unit, image_half = unit_rows(image_mantissa, image_exponent)
    factor = logit_scale[0]
    offset = logit_bias[0]
    z, x, c = lax.axis_index("z"), lax.axis_index("x"), lax.axis_index("core")

    texts = spread(text_half, "y", NY).reshape(NY * R, d)
    images = spread(image_half, "z", NZ).reshape(NZ * R, d)
    texts = jnp.concatenate([texts] + [shift(texts, "x", NX, k) for k in range(1, NX)], axis=0)
    texts = jnp.concatenate([texts, shift(texts, "core", NC, 1)], axis=0)

    place = positive.reshape(NZ, NX * NC, R)
    place = lax.dynamic_index_in_dim(place, x * NC + c, axis=1, keepdims=False).reshape(NZ * R)
    cs = (c + jnp.arange(NC, dtype=jnp.int32)[:, None, None]) % NC
    xs = (x + NX - jnp.arange(NX, dtype=jnp.int32)[None, :, None]) % NX
    yr = jnp.arange(NY * R, dtype=jnp.int32)[None, None, :]
    text_ids = (((z * NX + xs) * NC + cs) * (NY * R) + yr).reshape(NC * NX * NY * R)

    logits = factor * jnp.dot(images, texts.T, preferred_element_type=f32) + offset
    label_sign = jnp.where(place[:, None] == text_ids[None, :], 1.0, -1.0).astype(f32)
    weights = (-label_sign * jax.nn.sigmoid(-label_sign * logits)).astype(bf16)

    near = NX * NY * R
    far_part = (factor * jnp.dot(weights[:, near:].T, images, preferred_element_type=f32)).astype(bf16)
    far_part = shift(far_part, "core", NC, 1)
    part = (factor * jnp.dot(weights, texts, preferred_element_type=f32)).astype(bf16)
    part = exchange(part.reshape(NZ, R, d), "z")
    unit_grad_image = part.astype(f32).sum(axis=0)

    own = factor * jnp.dot(weights[:, :near].T, images, preferred_element_type=f32)
    own = (own + far_part.astype(f32)).astype(bf16).reshape(NX, NY * R, d)
    total = own[0].astype(f32)
    for k in range(1, NX):
        total = total + shift(own[k], "x", NX, -k).astype(f32)
    part = exchange(total.astype(bf16).reshape(NY, R, d), "y")
    unit_grad_text = part.astype(f32).sum(axis=0)

    return (
        tangent(unit_grad_image, image_unit, image_norm),
        tangent(unit_grad_text, text_unit, text_norm),
    )


def solution(mesh):
    fine = Mesh(mesh.devices.reshape(NY, NZ, NX, NC), AXES)
    image = ("y", "z", "x", "core")
    text = ("z", "x", "core", "y")
    return jax.shard_map(
        shards,
        mesh=fine,
        in_specs=(P(image, None), P(image), P(text, None), P(text), P("y"), P(), P()),
        out_specs=(P(image, None), P(text, None)),
        check_vma=False,
    )
```

```python
import jax
import jax.numpy as jnp
from jax import lax
from jax.experimental import pallas as pl
from jax.experimental.pallas import tpu as pltpu
from jax.sharding import Mesh, PartitionSpec as P

epsilon = 1e-06
AXES = ("y", "z", "x", "core")
NY, NZ, NX, NC = 8, 12, 4, 2
R = 8
f32 = jnp.float32
bf16 = jnp.bfloat16


def prologue_kernel(mantissa_ref, exponent_ref, out_ref, unit_ref, norm_ref):
    row = lax.broadcasted_iota(jnp.int32, (R, 1), 0)
    exponent = jnp.zeros((R, 1), jnp.int32)
    for r in range(R):
        exponent = jnp.where(row == r, exponent_ref[r], exponent)
    scaled = mantissa_ref[...].astype(f32) * jnp.exp2(exponent.astype(f32))
    norm = jnp.sqrt(jnp.sum(scaled * scaled, axis=1, keepdims=True) + epsilon)
    unit = scaled / norm
    norm_ref[...] = norm
    unit_ref[...] = unit
    half = unit.astype(bf16)
    for k in range(out_ref.shape[0]):
        out_ref[k] = half


def prologue(mantissa, exponent, copies):
    return pl.pallas_call(
        prologue_kernel,
        out_shape=(
            jax.ShapeDtypeStruct((copies,) + mantissa.shape, bf16),
            jax.ShapeDtypeStruct(mantissa.shape, f32),
            jax.ShapeDtypeStruct((R, 1), f32),
        ),
        in_specs=[
            pl.BlockSpec(memory_space=pltpu.VMEM),
            pl.BlockSpec(memory_space=pltpu.SMEM),
        ],
        out_specs=(pl.BlockSpec(memory_space=pltpu.VMEM),) * 3,
    )(mantissa, exponent)


def exchange(blocks, axis):
    return lax.all_to_all(blocks, axis, split_axis=0, concat_axis=0, tiled=True)


def shift(block, axis, n, k):
    return lax.ppermute(block, axis, [(i, (i + k) % n) for i in range(n)])


def product(a, b):
    return jnp.dot(a, b, preferred_element_type=f32)


def tangent(unit_grad, unit, norm):
    return (unit_grad - unit * jnp.sum(unit * unit_grad, axis=1, keepdims=True)) / norm


def shards(
    image_mantissa, image_exponent, text_mantissa, text_exponent, positive, logit_scale, logit_bias
):
    d = image_mantissa.shape[1]
    factor = logit_scale[0]
    offset = logit_bias[0]
    z, x, c = lax.axis_index("z"), lax.axis_index("x"), lax.axis_index("core")
    half_rows = NY * R
    near_rows = NX * half_rows

    place = positive.reshape(NZ, NX * NC, R)
    place = lax.dynamic_index_in_dim(place, x * NC + c, axis=1, keepdims=False).reshape(NZ * R)
    place = place - z * (NC * near_rows)
    place = jnp.where((place >= 0) & (place < NC * near_rows), place, -1)

    text_send, text_unit, text_norm = prologue(text_mantissa, text_exponent, NY)
    image_mantissa, place = lax.optimization_barrier((image_mantissa, place))
    image_send, image_unit, image_norm = prologue(image_mantissa, image_exponent, NZ)
    near_texts = lax.all_gather(exchange(text_send, "y").reshape(half_rows, d), "x", axis=0, tiled=True)
    far_texts = shift(near_texts, "core", NC, 1)
    images = exchange(image_send, "z").reshape(NZ * R, d)

    column = jnp.arange(near_rows, dtype=jnp.int32)[None, :]

    def weigh(texts, core):
        logits = factor * product(images, texts.T) + offset
        target = (column // half_rows) * (NC * half_rows) + core * half_rows + column % half_rows
        label_sign = jnp.where(place[:, None] == target, 1.0, -1.0).astype(f32)
        return (-label_sign * jax.nn.sigmoid(-label_sign * logits)).astype(bf16)

    far_weights = weigh(far_texts, 1 - c)
    far_part = (factor * product(far_weights.T, images)).astype(bf16)
    far_part = shift(far_part, "core", NC, 1)
    near_weights = weigh(near_texts, c)
    part = (factor * (product(near_weights, near_texts) + product(far_weights, far_texts))).astype(bf16)
    image_parts = exchange(part.reshape(NZ, R, d), "z")
    unit_grad_image = image_parts.astype(f32).sum(axis=0)

    near_part = factor * product(near_weights.T, images)
    near_part = (near_part + far_part.astype(f32)).astype(bf16).reshape(NX, half_rows, d)
    total = lax.dynamic_index_in_dim(near_part, x, axis=0, keepdims=False).astype(f32)
    for k in range(1, NX):
        block = lax.dynamic_index_in_dim(near_part, (x + k) % NX, axis=0, keepdims=False)
        total = total + shift(block, "x", NX, k).astype(f32)
    total = total.astype(bf16).reshape(NY, R, d)
    total, unit_grad_image = lax.optimization_barrier((total, unit_grad_image))
    unit_grad_text = exchange(total, "y").astype(f32).sum(axis=0)

    return (
        tangent(unit_grad_image, image_unit, image_norm),
        tangent(unit_grad_text, text_unit, text_norm),
    )


def solution(mesh):
    fine = Mesh(mesh.devices.reshape(NY, NZ, NX, NC), AXES)
    image = ("y", "z", "x", "core")
    text = ("z", "x", "core", "y")
    return jax.shard_map(
        shards,
        mesh=fine,
        in_specs=(P(image, None), P(image), P(text, None), P(text), P("y"), P(), P()),
        out_specs=(P(image, None), P(text, None)),
        check_vma=False,
    )
```

```python
import jax
import jax.numpy as jnp
from jax import lax
from jax.experimental import pallas as pl
from jax.experimental.pallas import tpu as pltpu
from jax.sharding import Mesh, PartitionSpec as P

epsilon = 1e-06
AXES = ("y", "z", "x", "core")
NY, NZ, NX, NC = 8, 12, 4, 2
R = 8
f32 = jnp.float32
bf16 = jnp.bfloat16


def unit_rows(mantissa_ref, exponent_ref):
    row = lax.broadcasted_iota(jnp.int32, (R, 1), 0)
    exponent = jnp.zeros((R, 1), jnp.int32)
    for r in range(R):
        exponent = jnp.where(row == r, exponent_ref[r], exponent)
    scaled = mantissa_ref[...].astype(f32) * jnp.exp2(exponent.astype(f32))
    norm = jnp.sqrt(jnp.sum(scaled * scaled, axis=1, keepdims=True) + epsilon)
    return norm, scaled / norm


def text_kernel(mantissa_ref, exponent_ref, send_ref):
    _, unit = unit_rows(mantissa_ref, exponent_ref)
    half = unit.astype(bf16)
    for k in range(NY):
        send_ref[k] = half


def image_kernel(
    image_ref, image_exponent_ref, text_ref, text_exponent_ref, scale_ref, bias_ref,
    send_ref, image_unit_ref, image_gain_ref, text_unit_ref, text_gain_ref, scale_row_ref, bias_row_ref,
):
    norm, unit = unit_rows(image_ref, image_exponent_ref)
    half = unit.astype(bf16)
    for k in range(NZ):
        send_ref[k] = half
    factor = scale_ref[0]
    image_unit_ref[...] = unit
    image_gain_ref[...] = jnp.broadcast_to(factor / norm, unit.shape)
    norm, unit = unit_rows(text_ref, text_exponent_ref)
    text_unit_ref[...] = unit
    text_gain_ref[...] = jnp.broadcast_to(factor / norm, unit.shape)
    scale_row_ref[...] = jnp.full(scale_row_ref.shape, factor, f32)
    bias_row_ref[...] = jnp.full(bias_row_ref.shape, bias_ref[0], f32)


vmem = pl.BlockSpec(memory_space=pltpu.VMEM)
smem = pl.BlockSpec(memory_space=pltpu.SMEM)


def text_prologue(mantissa, exponent):
    return pl.pallas_call(
        text_kernel,
        out_shape=jax.ShapeDtypeStruct((NY,) + mantissa.shape, bf16),
        in_specs=[vmem, smem],
        out_specs=vmem,
    )(mantissa, exponent)


def image_prologue(image, image_exponent, text, text_exponent, scale, bias):
    d = image.shape[1]
    rows = jax.ShapeDtypeStruct((R, d), f32)
    row = jax.ShapeDtypeStruct((1, NX * NY * R), f32)
    return pl.pallas_call(
        image_kernel,
        out_shape=(
            jax.ShapeDtypeStruct((NZ, R, d), bf16), rows, rows, rows, rows, row, row,
        ),
        in_specs=[vmem, smem, vmem, smem, smem, smem],
        out_specs=(vmem,) * 7,
    )(image, image_exponent, text, text_exponent, scale, bias)


def exchange(blocks, axis):
    return lax.all_to_all(blocks, axis, split_axis=0, concat_axis=0, tiled=True)


def shift(block, axis, n, k):
    return lax.ppermute(block, axis, [(i, (i + k) % n) for i in range(n)])


def rows_at(array, start, size):
    starts = (start,) + (jnp.int32(0),) * (array.ndim - 1)
    return lax.dynamic_slice(array, starts, (size,) + array.shape[1:], allow_negative_indices=False)


def product(a, b):
    return jnp.dot(a, b, preferred_element_type=f32)


def tangent(unit_grad, unit, gain):
    return (unit_grad - unit * jnp.sum(unit * unit_grad, axis=1, keepdims=True)) * gain


def shards(
    image_mantissa, image_exponent, text_mantissa, text_exponent, positive, logit_scale, logit_bias
):
    d = image_mantissa.shape[1]
    z, x, c = lax.axis_index("z"), lax.axis_index("x"), lax.axis_index("core")
    half_rows = NY * R
    near_rows = NX * half_rows
    own = NZ * R

    place = positive.reshape(NZ, NX, NC, R).transpose(1, 2, 0, 3).reshape(NX, NC * own)
    place = rows_at(place, x, 1).reshape(NC * own)
    place = place - (z * (NC * near_rows) + c * half_rows)
    place = jnp.where((place >= 0) & (place < NC * near_rows), place, -1)

    text_send = text_prologue(text_mantissa, text_exponent)
    image_mantissa, place = lax.optimization_barrier((image_mantissa, place))
    image_send, image_unit, image_gain, text_unit, text_gain, scale, bias = image_prologue(
        image_mantissa, image_exponent, text_mantissa, text_exponent, logit_scale, logit_bias
    )
    texts = lax.all_gather(exchange(text_send, "y").reshape(half_rows, d), "x", axis=0, tiled=True)
    images = lax.all_gather(exchange(image_send, "z").reshape(own, d), "core", axis=0, tiled=True)

    column = jnp.arange(near_rows, dtype=jnp.int32)[None, :]
    target = (column // half_rows) * (NC * half_rows) + column % half_rows
    logits = scale * product(images, texts.T) + bias
    label_sign = jnp.where(place[:, None] == target, 1.0, -1.0).astype(f32)
    weights = (-label_sign * jax.nn.sigmoid(-label_sign * logits)).astype(bf16)

    far = rows_at(weights, (1 - c) * own, own)
    near = rows_at(weights, c * own, own)
    far = product(far, texts).astype(bf16)
    far, weights = lax.optimization_barrier((far, weights))
    far = shift(far, "core", NC, 1)

    part = product(weights.T, images).astype(bf16).reshape(NX, half_rows, d)
    blocks = [rows_at(part, (x + k) & (NX - 1), 1).reshape(half_rows, d) for k in range(NX)]
    opposite = shift(blocks[2], "x", NX, 2)

    near = lax.optimization_barrier(product(near, texts))
    image_part = (near + far.astype(f32)).astype(bf16)
    image_part, blocks[1], blocks[3] = lax.optimization_barrier((image_part, blocks[1], blocks[3]))
    image_parts = exchange(image_part.reshape(NZ, R, d), "z")
    unit_grad_image = image_parts.astype(f32).sum(axis=0)

    total = blocks[0].astype(f32) + opposite.astype(f32)
    total = total + shift(blocks[1], "x", NX, 1).astype(f32) + shift(blocks[3], "x", NX, 3).astype(f32)
    total = total.astype(bf16).reshape(NY, R, d)
    total, unit_grad_image = lax.optimization_barrier((total, unit_grad_image))
    unit_grad_text = exchange(total, "y").astype(f32).sum(axis=0)

    return (
        tangent(unit_grad_image, image_unit, image_gain),
        tangent(unit_grad_text, text_unit, text_gain),
    )


def solution(mesh):
    fine = Mesh(mesh.devices.reshape(NY, NZ, NX, NC), AXES)
    image = ("y", "z", "x", "core")
    text = ("z", "x", "core", "y")
    return jax.shard_map(
        shards,
        mesh=fine,
        in_specs=(P(image, None), P(image), P(text, None), P(text), P("y"), P(), P()),
        out_specs=(P(image, None), P(text, None)),
        check_vma=False,
    )
```

```python
import jax
import jax.numpy as jnp
from jax import lax
from jax.experimental import pallas as pl
from jax.experimental.pallas import tpu as pltpu
from jax.sharding import Mesh, PartitionSpec as P

epsilon = 1e-06
AXES = ("y", "z", "x", "core")
NY, NZ, NX, NC = 8, 12, 4, 2
R = 8
f32 = jnp.float32
bf16 = jnp.bfloat16


def unit_rows(mantissa_ref, exponent_ref):
    row = lax.broadcasted_iota(jnp.int32, (R, 1), 0)
    exponent = jnp.zeros((R, 1), jnp.int32)
    for r in range(R):
        exponent = jnp.where(row == r, exponent_ref[r], exponent)
    scaled = mantissa_ref[...].astype(f32) * jnp.exp2(exponent.astype(f32))
    norm = jnp.sqrt(jnp.sum(scaled * scaled, axis=1, keepdims=True) + epsilon)
    return norm, scaled / norm


def text_kernel(mantissa_ref, exponent_ref, send_ref):
    _, unit = unit_rows(mantissa_ref, exponent_ref)
    half = unit.astype(bf16)
    for k in range(NY):
        send_ref[k] = half


def image_kernel(
    image_ref, image_exponent_ref, text_ref, text_exponent_ref, scale_ref, bias_ref,
    send_ref, image_unit_ref, image_gain_ref, text_unit_ref, text_gain_ref, scale_row_ref, bias_row_ref,
):
    norm, unit = unit_rows(image_ref, image_exponent_ref)
    half = unit.astype(bf16)
    for k in range(NZ):
        send_ref[k] = half
    factor = scale_ref[0]
    image_unit_ref[...] = unit
    image_gain_ref[...] = jnp.broadcast_to(factor / norm, unit.shape)
    norm, unit = unit_rows(text_ref, text_exponent_ref)
    text_unit_ref[...] = unit
    text_gain_ref[...] = jnp.broadcast_to(factor / norm, unit.shape)
    scale_row_ref[...] = jnp.full(scale_row_ref.shape, factor, f32)
    bias_row_ref[...] = jnp.full(bias_row_ref.shape, bias_ref[0], f32)


vmem = pl.BlockSpec(memory_space=pltpu.VMEM)
smem = pl.BlockSpec(memory_space=pltpu.SMEM)


def text_prologue(mantissa, exponent):
    return pl.pallas_call(
        text_kernel,
        out_shape=jax.ShapeDtypeStruct((NY,) + mantissa.shape, bf16),
        in_specs=[vmem, smem],
        out_specs=vmem,
    )(mantissa, exponent)


def image_prologue(image, image_exponent, text, text_exponent, scale, bias):
    d = image.shape[1]
    rows = jax.ShapeDtypeStruct((R, d), f32)
    row = jax.ShapeDtypeStruct((1, NX * NY * R), f32)
    return pl.pallas_call(
        image_kernel,
        out_shape=(
            jax.ShapeDtypeStruct((NZ, R, d), bf16), rows, rows, rows, rows, row, row,
        ),
        in_specs=[vmem, smem, vmem, smem, smem, smem],
        out_specs=(vmem,) * 7,
    )(image, image_exponent, text, text_exponent, scale, bias)


def exchange(blocks, axis):
    return lax.all_to_all(blocks, axis, split_axis=0, concat_axis=0, tiled=True)


def shift(block, axis, n, k):
    return lax.ppermute(block, axis, [(i, (i + k) % n) for i in range(n)])


def cross(block, k):
    moves = [(x * NC + c, (x + (k if c == 0 else -k)) % NX * NC + c) for x in range(NX) for c in range(NC)]
    return lax.ppermute(block, ("x", "core"), moves)


def rows_at(array, start, size):
    starts = (start,) + (jnp.int32(0),) * (array.ndim - 1)
    return lax.dynamic_slice(array, starts, (size,) + array.shape[1:], allow_negative_indices=False)


def product(a, b):
    return jnp.dot(a, b, preferred_element_type=f32)


def tangent(unit_grad, unit, gain):
    return (unit_grad - unit * jnp.sum(unit * unit_grad, axis=1, keepdims=True)) * gain


def shards(
    image_mantissa, image_exponent, text_mantissa, text_exponent, positive, logit_scale, logit_bias
):
    d = image_mantissa.shape[1]
    z, x, c = lax.axis_index("z"), lax.axis_index("x"), lax.axis_index("core")
    half_rows = NY * R
    near_rows = NX * half_rows
    own = NZ * R

    place = positive.reshape(NZ, NX, NC, R).transpose(1, 2, 0, 3).reshape(NX, NC * own)
    place = rows_at(place, x, 1).reshape(NC * own)
    place = place - (z * (NC * near_rows) + c * half_rows)
    place = jnp.where((place >= 0) & (place < NC * near_rows), place, -1)

    text_send = text_prologue(text_mantissa, text_exponent)
    image_mantissa, place = lax.optimization_barrier((image_mantissa, place))
    image_send, image_unit, image_gain, text_unit, text_gain, scale, bias = image_prologue(
        image_mantissa, image_exponent, text_mantissa, text_exponent, logit_scale, logit_bias
    )
    texts = lax.all_gather(exchange(text_send, "y").reshape(half_rows, d), "x", axis=0, tiled=True)
    images = lax.all_gather(exchange(image_send, "z").reshape(own, d), "core", axis=0, tiled=True)

    column = jnp.arange(near_rows, dtype=jnp.int32)[None, :]
    target = (column // half_rows) * (NC * half_rows) + column % half_rows
    logits = scale * product(images, texts.T) + bias
    label_sign = jnp.where(place[:, None] == target, 1.0, -1.0).astype(f32)
    weights = (-label_sign * jax.nn.sigmoid(-label_sign * logits)).astype(bf16)

    far = rows_at(weights, (1 - c) * own, own)
    near = rows_at(weights, c * own, own)
    far = product(far, texts).astype(bf16)
    far, weights = lax.optimization_barrier((far, weights))
    far = shift(far, "core", NC, 1)

    part = product(weights.T, images).astype(bf16).reshape(NX, half_rows, d)
    ways = (0, 1 + 2 * c, 2, 3 - 2 * c)
    blocks = [rows_at(part, (x + k) & (NX - 1), 1).reshape(half_rows, d) for k in ways]
    near = lax.optimization_barrier(product(near, texts))
    image_part = (near + far.astype(f32)).astype(bf16)
    image_part, *blocks = lax.optimization_barrier((image_part, *blocks))
    image_parts = exchange(image_part.reshape(NZ, R, d), "z")
    unit_grad_image = image_parts.astype(f32).sum(axis=0)

    opposite = shift(blocks[2], "x", NX, 2)
    total = blocks[0].astype(f32) + opposite.astype(f32)
    total = total + cross(blocks[1], 1).astype(f32) + cross(blocks[3], 3).astype(f32)
    total = total.astype(bf16).reshape(NY, R, d)
    image_grad = tangent(unit_grad_image, image_unit, image_gain)
    total, image_grad = lax.optimization_barrier((total, image_grad))
    unit_grad_text = exchange(total, "y").astype(f32).sum(axis=0)

    return image_grad, tangent(unit_grad_text, text_unit, text_gain)


def solution(mesh):
    fine = Mesh(mesh.devices.reshape(NY, NZ, NX, NC), AXES)
    image = ("y", "z", "x", "core")
    text = ("z", "x", "core", "y")
    return jax.shard_map(
        shards,
        mesh=fine,
        in_specs=(P(image, None), P(image), P(text, None), P(text), P("y"), P(), P()),
        out_specs=(P(image, None), P(text, None)),
        check_vma=False,
    )
```

```python
import jax
import jax.numpy as jnp
from jax import lax
from jax.experimental import pallas as pl
from jax.experimental.pallas import tpu as pltpu
from jax.sharding import Mesh, PartitionSpec as P

epsilon = 1e-06
AXES = ("y", "z", "x", "core")
NY, NZ, NX, NC = 8, 12, 4, 2
R = 8
f32 = jnp.float32
bf16 = jnp.bfloat16


def unit_rows(mantissa_ref, exponent_ref):
    row = lax.broadcasted_iota(jnp.int32, (R, 1), 0)
    exponent = jnp.zeros((R, 1), jnp.int32)
    for r in range(R):
        exponent = jnp.where(row == r, exponent_ref[r], exponent)
    scaled = mantissa_ref[...].astype(f32) * jnp.exp2(exponent.astype(f32))
    norm = jnp.sqrt(jnp.sum(scaled * scaled, axis=1, keepdims=True) + epsilon)
    return norm, scaled / norm


def text_kernel(mantissa_ref, exponent_ref, send_ref):
    _, unit = unit_rows(mantissa_ref, exponent_ref)
    half = unit.astype(bf16)
    for k in range(NY):
        send_ref[k] = half


def image_kernel(
    image_ref, image_exponent_ref, text_ref, text_exponent_ref, scale_ref, bias_ref,
    send_ref, image_unit_ref, image_gain_ref, text_unit_ref, text_gain_ref, scale_row_ref, bias_row_ref,
):
    norm, unit = unit_rows(image_ref, image_exponent_ref)
    half = unit.astype(bf16)
    for k in range(NZ):
        send_ref[k] = half
    factor = scale_ref[0]
    image_unit_ref[...] = unit
    image_gain_ref[...] = jnp.broadcast_to(factor / norm, unit.shape)
    norm, unit = unit_rows(text_ref, text_exponent_ref)
    text_unit_ref[...] = unit
    text_gain_ref[...] = jnp.broadcast_to(factor / norm, unit.shape)
    scale_row_ref[...] = jnp.full(scale_row_ref.shape, factor, f32)
    bias_row_ref[...] = jnp.full(bias_row_ref.shape, bias_ref[0], f32)


vmem = pl.BlockSpec(memory_space=pltpu.VMEM)
smem = pl.BlockSpec(memory_space=pltpu.SMEM)


def text_prologue(mantissa, exponent):
    return pl.pallas_call(
        text_kernel,
        out_shape=jax.ShapeDtypeStruct((NY,) + mantissa.shape, bf16),
        in_specs=[vmem, smem],
        out_specs=vmem,
    )(mantissa, exponent)


def image_prologue(image, image_exponent, text, text_exponent, scale, bias):
    d = image.shape[1]
    rows = jax.ShapeDtypeStruct((R, d), f32)
    row = jax.ShapeDtypeStruct((1, NX * NY * R), f32)
    return pl.pallas_call(
        image_kernel,
        out_shape=(
            jax.ShapeDtypeStruct((NZ, R, d), bf16), rows, rows, rows, rows, row, row,
        ),
        in_specs=[vmem, smem, vmem, smem, smem, smem],
        out_specs=(vmem,) * 7,
    )(image, image_exponent, text, text_exponent, scale, bias)


def exchange(blocks, axis):
    return lax.all_to_all(blocks, axis, split_axis=0, concat_axis=0, tiled=True)


def shift(block, axis, n, k):
    return lax.ppermute(block, axis, [(i, (i + k) % n) for i in range(n)])


def cross(block, k):
    moves = [(x * NC + c, (x + (k if c == 0 else -k)) % NX * NC + c) for x in range(NX) for c in range(NC)]
    return lax.ppermute(block, ("x", "core"), moves)


def rows_at(array, start, size):
    starts = (start,) + (jnp.int32(0),) * (array.ndim - 1)
    return lax.dynamic_slice(array, starts, (size,) + array.shape[1:], allow_negative_indices=False)


def product(a, b):
    return jnp.dot(a, b, preferred_element_type=f32)


def tangent(unit_grad, unit, gain):
    return (unit_grad - unit * jnp.sum(unit * unit_grad, axis=1, keepdims=True)) * gain


def shards(
    image_mantissa, image_exponent, text_mantissa, text_exponent, positive, logit_scale, logit_bias
):
    d = image_mantissa.shape[1]
    z, x, c = lax.axis_index("z"), lax.axis_index("x"), lax.axis_index("core")
    half_rows = NY * R
    near_rows = NX * half_rows
    own = NZ * R

    place = positive.reshape(NZ, NX * NC, R).transpose(1, 0, 2).reshape(NX * NC, own)
    place = place - z * (NX * NC * half_rows)
    far_place = rows_at(place, x * NC + 1 - c, 1).reshape(own)
    place = rows_at(place, x * NC + c, 1).reshape(own)

    text_send = text_prologue(text_mantissa, text_exponent)
    image_mantissa, place, far_place = lax.optimization_barrier((image_mantissa, place, far_place))
    image_send, image_unit, image_gain, text_unit, text_gain, scale, bias = image_prologue(
        image_mantissa, image_exponent, text_mantissa, text_exponent, logit_scale, logit_bias
    )
    texts = lax.all_gather(exchange(text_send, "y").reshape(half_rows, d), "x", axis=0, tiled=True)
    far_texts = shift(texts, "core", NC, 1)
    images = exchange(image_send, "z").reshape(own, d)
    far_images = shift(images, "core", NC, 1)

    column = jnp.arange(near_rows, dtype=jnp.int32)[None, :]

    def weigh(images, place, texts, core):
        target = (column // half_rows * NC + core) * half_rows + column % half_rows
        logits = scale * product(images, texts.T) + bias
        label_sign = jnp.where(place[:, None] == target, 1.0, -1.0).astype(f32)
        return (-label_sign * jax.nn.sigmoid(-label_sign * logits)).astype(bf16)

    weights = weigh(images, place, texts, c)
    near = lax.optimization_barrier(product(weights, texts))
    cross_weights = weigh(images, place, far_texts, 1 - c)
    image_part = (near + product(cross_weights, far_texts)).astype(bf16)

    image_part, far_images = lax.optimization_barrier((image_part, far_images))
    far_weights = weigh(far_images, far_place, texts, c)
    weights = jnp.concatenate([weights, far_weights], axis=0)
    images = jnp.concatenate([images, far_images], axis=0)
    part = product(weights.T, images).astype(bf16).reshape(NX, half_rows, d)
    ways = (0, 1 + 2 * c, 2, 3 - 2 * c)
    blocks = [rows_at(part, (x + k) & (NX - 1), 1).reshape(half_rows, d) for k in ways]
    image_parts = exchange(image_part.reshape(NZ, R, d), "z")
    unit_grad_image = image_parts.astype(f32).sum(axis=0)

    opposite = shift(blocks[2], "x", NX, 2)
    total = blocks[0].astype(f32) + opposite.astype(f32)
    total = total + cross(blocks[1], 1).astype(f32) + cross(blocks[3], 3).astype(f32)
    total = total.astype(bf16).reshape(NY, R, d)
    image_grad = tangent(unit_grad_image, image_unit, image_gain)
    total, image_grad = lax.optimization_barrier((total, image_grad))
    unit_grad_text = exchange(total, "y").astype(f32).sum(axis=0)

    return image_grad, tangent(unit_grad_text, text_unit, text_gain)


def solution(mesh):
    fine = Mesh(mesh.devices.reshape(NY, NZ, NX, NC), AXES)
    image = ("y", "z", "x", "core")
    text = ("z", "x", "core", "y")
    return jax.shard_map(
        shards,
        mesh=fine,
        in_specs=(P(image, None), P(image), P(text, None), P(text), P("y"), P(), P()),
        out_specs=(P(image, None), P(text, None)),
        check_vma=False,
    )
```

```python
import jax
import jax.numpy as jnp
from jax import lax
from jax.experimental import pallas as pl
from jax.experimental.pallas import tpu as pltpu
from jax.sharding import Mesh, PartitionSpec as P

epsilon = 1e-06
AXES = ("y", "z", "x", "core")
NY, NZ, NX, NC = 8, 12, 4, 2
FIRST_Y, FIRST_Z = 4, 11
R = 8
f32 = jnp.float32
bf16 = jnp.bfloat16


def unit_rows(mantissa_ref, exponent_ref):
    row = lax.broadcasted_iota(jnp.int32, (R, 1), 0)
    exponent = jnp.zeros((R, 1), jnp.int32)
    for r in range(R):
        exponent = jnp.where(row == r, exponent_ref[r], exponent)
    scaled = mantissa_ref[...].astype(f32) * jnp.exp2(exponent.astype(f32))
    norm = jnp.sqrt(jnp.sum(scaled * scaled, axis=1, keepdims=True) + epsilon)
    return norm, scaled / norm


def text_kernel(mantissa_ref, exponent_ref, send_ref):
    _, unit = unit_rows(mantissa_ref, exponent_ref)
    half = unit.astype(bf16)
    for k in range(NY):
        send_ref[k] = half


def image_kernel(
    image_ref, image_exponent_ref, text_ref, text_exponent_ref, scale_ref, bias_ref,
    send_ref, image_unit_ref, image_gain_ref, text_unit_ref, text_gain_ref, scale_row_ref, bias_row_ref,
):
    norm, unit = unit_rows(image_ref, image_exponent_ref)
    half = unit.astype(bf16)
    for k in range(NZ):
        send_ref[k] = half
    factor = scale_ref[0]
    image_unit_ref[...] = unit
    image_gain_ref[...] = jnp.broadcast_to(factor / norm, unit.shape)
    norm, unit = unit_rows(text_ref, text_exponent_ref)
    text_unit_ref[...] = unit
    text_gain_ref[...] = jnp.broadcast_to(factor / norm, unit.shape)
    scale_row_ref[...] = jnp.full(scale_row_ref.shape, factor, f32)
    bias_row_ref[...] = jnp.full(bias_row_ref.shape, bias_ref[0], f32)


vmem = pl.BlockSpec(memory_space=pltpu.VMEM)
smem = pl.BlockSpec(memory_space=pltpu.SMEM)


def text_prologue(mantissa, exponent):
    return pl.pallas_call(
        text_kernel,
        out_shape=jax.ShapeDtypeStruct((NY,) + mantissa.shape, bf16),
        in_specs=[vmem, smem],
        out_specs=vmem,
    )(mantissa, exponent)


def image_prologue(image, image_exponent, text, text_exponent, scale, bias):
    d = image.shape[1]
    rows = jax.ShapeDtypeStruct((R, d), f32)
    row = jax.ShapeDtypeStruct((1, NX * NY * R), f32)
    return pl.pallas_call(
        image_kernel,
        out_shape=(
            jax.ShapeDtypeStruct((NZ, R, d), bf16), rows, rows, rows, rows, row, row,
        ),
        in_specs=[vmem, smem, vmem, smem, smem, smem],
        out_specs=(vmem,) * 7,
    )(image, image_exponent, text, text_exponent, scale, bias)


def exchange(blocks, axis, first=0):
    n = blocks.shape[0]
    order = [[(first + k) % n for k in range(n)]]
    return lax.all_to_all(blocks, axis, split_axis=0, concat_axis=0, axis_index_groups=order, tiled=True)


def shift(block, axis, n, k):
    return lax.ppermute(block, axis, [(i, (i + k) % n) for i in range(n)])


def cross(block, k):
    moves = [(x * NC + c, (x + (k if c == 0 else -k)) % NX * NC + c) for x in range(NX) for c in range(NC)]
    return lax.ppermute(block, ("x", "core"), moves)


def rows_at(array, start, size):
    starts = (start,) + (jnp.int32(0),) * (array.ndim - 1)
    return lax.dynamic_slice(array, starts, (size,) + array.shape[1:], allow_negative_indices=False)


def product(a, b):
    return jnp.dot(a, b, preferred_element_type=f32)


def tangent(unit_grad, unit, gain):
    return (unit_grad - unit * jnp.sum(unit * unit_grad, axis=1, keepdims=True)) * gain


def shards(
    image_mantissa, image_exponent, text_mantissa, text_exponent, positive, logit_scale, logit_bias
):
    d = image_mantissa.shape[1]
    z, x, c = lax.axis_index("z"), lax.axis_index("x"), lax.axis_index("core")
    half_rows = NY * R
    near_rows = NX * half_rows
    own = NZ * R

    place = positive.reshape(NZ, NX * NC, R).transpose(1, 0, 2).reshape(NX * NC, own)
    place = place - z * (NX * NC * half_rows)
    far_place = jnp.roll(rows_at(place, x * NC + 1 - c, 1).reshape(own), -FIRST_Z * R)
    place = jnp.roll(rows_at(place, x * NC + c, 1).reshape(own), -FIRST_Z * R)

    text_send = text_prologue(text_mantissa, text_exponent)
    image_mantissa, place, far_place = lax.optimization_barrier((image_mantissa, place, far_place))
    image_send, image_unit, image_gain, text_unit, text_gain, scale, bias = image_prologue(
        image_mantissa, image_exponent, text_mantissa, text_exponent, logit_scale, logit_bias
    )
    texts = lax.all_gather(exchange(text_send, "y", FIRST_Y).reshape(half_rows, d), "x", axis=0, tiled=True)
    far_texts = shift(texts, "core", NC, 1)
    images = exchange(image_send, "z", FIRST_Z).reshape(own, d)
    far_images = shift(images, "core", NC, 1)

    column = jnp.arange(near_rows, dtype=jnp.int32)[None, :]

    def weigh(images, place, texts, core):
        target = (column // half_rows * NC + core) * half_rows + (column + FIRST_Y * R) % half_rows
        logits = scale * product(images, texts.T) + bias
        label_sign = jnp.where(place[:, None] == target, 1.0, -1.0).astype(f32)
        return (-label_sign * jax.nn.sigmoid(-label_sign * logits)).astype(bf16)

    weights = weigh(images, place, texts, c)
    near = lax.optimization_barrier(product(jnp.roll(weights, (FIRST_Z - 3) * R, axis=0), texts))
    cross_weights = jnp.roll(weigh(images, place, far_texts, 1 - c), (FIRST_Z - 3) * R, axis=0)
    image_part = (near + product(cross_weights, far_texts)).astype(bf16)

    image_part, far_images = lax.optimization_barrier((image_part, far_images))
    far_weights = weigh(far_images, far_place, texts, c)
    weights = jnp.concatenate([weights, far_weights], axis=0)
    images = jnp.concatenate([images, far_images], axis=0)
    part = product(weights.T, images).astype(bf16).reshape(NX, half_rows, d)
    ways = (0, 1 + 2 * c, 2, 3 - 2 * c)
    blocks = [rows_at(part, (x + k) & (NX - 1), 1).reshape(half_rows, d) for k in ways]
    image_parts = exchange(image_part.reshape(NZ, R, d), "z", 3)
    unit_grad_image = image_parts.astype(f32).sum(axis=0)

    opposite = shift(blocks[2], "x", NX, 2)
    total = blocks[0].astype(f32) + opposite.astype(f32)
    total = total + cross(blocks[1], 1).astype(f32) + cross(blocks[3], 3).astype(f32)
    total = total.astype(bf16).reshape(NY, R, d)
    image_grad = tangent(unit_grad_image, image_unit, image_gain)
    total, image_grad = lax.optimization_barrier((total, image_grad))
    unit_grad_text = exchange(total, "y", FIRST_Y).astype(f32).sum(axis=0)

    return image_grad, tangent(unit_grad_text, text_unit, text_gain)


def solution(mesh):
    fine = Mesh(mesh.devices.reshape(NY, NZ, NX, NC), AXES)
    image = ("y", "z", "x", "core")
    text = ("z", "x", "core", "y")
    return jax.shard_map(
        shards,
        mesh=fine,
        in_specs=(P(image, None), P(image), P(text, None), P(text), P("y"), P(), P()),
        out_specs=(P(image, None), P(text, None)),
        check_vma=False,
    )
```

```python
import jax
import jax.numpy as jnp
from jax import lax
from jax.experimental import pallas as pl
from jax.experimental.pallas import tpu as pltpu
from jax.sharding import Mesh, PartitionSpec as P

epsilon = 1e-06
AXES = ("y", "z", "x", "core")
NY, NZ, NX, NC = 8, 12, 4, 2
FIRST_Y, FIRST_Z = 4, 11
R = 8
f32 = jnp.float32
bf16 = jnp.bfloat16


def unit_rows(mantissa_ref, exponent_ref):
    row = lax.broadcasted_iota(jnp.int32, (R, 1), 0)
    exponent = jnp.zeros((R, 1), jnp.int32)
    for r in range(R):
        exponent = jnp.where(row == r, exponent_ref[r], exponent)
    scaled = mantissa_ref[...].astype(f32) * jnp.exp2(exponent.astype(f32))
    norm = jnp.sqrt(jnp.sum(scaled * scaled, axis=1, keepdims=True) + epsilon)
    return norm, scaled / norm


def text_kernel(mantissa_ref, exponent_ref, send_ref):
    _, unit = unit_rows(mantissa_ref, exponent_ref)
    half = unit.astype(bf16)
    for k in range(NY):
        send_ref[k] = half


def image_kernel(
    image_ref, image_exponent_ref, text_ref, text_exponent_ref, scale_ref, bias_ref,
    send_ref, image_unit_ref, image_gain_ref, text_unit_ref, text_gain_ref, scale_row_ref, bias_row_ref,
):
    norm, unit = unit_rows(image_ref, image_exponent_ref)
    half = unit.astype(bf16)
    for k in range(NZ):
        send_ref[k] = half
    factor = scale_ref[0]
    image_unit_ref[...] = unit
    image_gain_ref[...] = jnp.broadcast_to(factor / norm, unit.shape)
    norm, unit = unit_rows(text_ref, text_exponent_ref)
    text_unit_ref[...] = unit
    text_gain_ref[...] = jnp.broadcast_to(factor / norm, unit.shape)
    scale_row_ref[...] = jnp.full(scale_row_ref.shape, factor, f32)
    bias_row_ref[...] = jnp.full(bias_row_ref.shape, bias_ref[0], f32)


vmem = pl.BlockSpec(memory_space=pltpu.VMEM)
smem = pl.BlockSpec(memory_space=pltpu.SMEM)


def text_prologue(mantissa, exponent):
    return pl.pallas_call(
        text_kernel,
        out_shape=jax.ShapeDtypeStruct((NY,) + mantissa.shape, bf16),
        in_specs=[vmem, smem],
        out_specs=vmem,
    )(mantissa, exponent)


def image_prologue(image, image_exponent, text, text_exponent, scale, bias):
    d = image.shape[1]
    rows = jax.ShapeDtypeStruct((R, d), f32)
    row = jax.ShapeDtypeStruct((1, NX * NY * R), f32)
    return pl.pallas_call(
        image_kernel,
        out_shape=(
            jax.ShapeDtypeStruct((NZ, R, d), bf16), rows, rows, rows, rows, row, row,
        ),
        in_specs=[vmem, smem, vmem, smem, smem, smem],
        out_specs=(vmem,) * 7,
    )(image, image_exponent, text, text_exponent, scale, bias)


def exchange(blocks, axis, first=0):
    n = blocks.shape[0]
    order = [[(first + k) % n for k in range(n)]]
    return lax.all_to_all(blocks, axis, split_axis=0, concat_axis=0, axis_index_groups=order, tiled=True)


def shift(block, axis, n, k):
    return lax.ppermute(block, axis, [(i, (i + k) % n) for i in range(n)])


def cross(block, k):
    moves = [(x * NC + c, (x + (k if c == 0 else -k)) % NX * NC + c) for x in range(NX) for c in range(NC)]
    return lax.ppermute(block, ("x", "core"), moves)


def rows_at(array, start, size):
    starts = (start,) + (jnp.int32(0),) * (array.ndim - 1)
    return lax.dynamic_slice(array, starts, (size,) + array.shape[1:], allow_negative_indices=False)


def product(a, b):
    return jnp.dot(a, b, preferred_element_type=f32)


def tangent(unit_grad, unit, gain):
    return (unit_grad - unit * jnp.sum(unit * unit_grad, axis=1, keepdims=True)) * gain


def shards(
    image_mantissa, image_exponent, text_mantissa, text_exponent, positive, logit_scale, logit_bias
):
    d = image_mantissa.shape[1]
    z, x, c = lax.axis_index("z"), lax.axis_index("x"), lax.axis_index("core")
    half_rows = NY * R
    near_rows = NX * half_rows
    own = NZ * R

    place = positive.reshape(NZ, NX * NC, R).transpose(1, 0, 2).reshape(NX * NC, own)
    place = place - z * (NX * NC * half_rows)
    far_place = jnp.roll(rows_at(place, x * NC + 1 - c, 1).reshape(own), -FIRST_Z * R)
    place = jnp.roll(rows_at(place, x * NC + c, 1).reshape(own), -FIRST_Z * R)

    text_send = text_prologue(text_mantissa, text_exponent)
    image_mantissa, place, far_place = lax.optimization_barrier((image_mantissa, place, far_place))
    image_send, image_unit, image_gain, text_unit, text_gain, scale, bias = image_prologue(
        image_mantissa, image_exponent, text_mantissa, text_exponent, logit_scale, logit_bias
    )
    texts = lax.all_gather(exchange(text_send, "y", FIRST_Y).reshape(half_rows, d), "x", axis=0, tiled=True)
    far_texts = shift(texts, "core", NC, 1)
    images = exchange(image_send, "z", FIRST_Z).reshape(own, d)
    far_images = shift(images, "core", NC, 1)

    column = jnp.arange(near_rows, dtype=jnp.int32)[None, :]

    def weigh(images, place, texts, core):
        target = (column // half_rows * NC + core) * half_rows + (column + FIRST_Y * R) % half_rows
        logits = scale * product(images, texts.T) + bias
        label_sign = jnp.where(place[:, None] == target, 1.0, -1.0).astype(f32)
        return (-label_sign * jax.nn.sigmoid(-label_sign * logits)).astype(bf16)

    weights = weigh(images, place, texts, c)
    near = lax.optimization_barrier(product(jnp.roll(weights, (FIRST_Z - 3) * R, axis=0), texts))
    cross_weights = jnp.roll(weigh(images, place, far_texts, 1 - c), (FIRST_Z - 3) * R, axis=0)
    image_part = (near + product(cross_weights, far_texts)).astype(bf16)

    image_part, far_images = lax.optimization_barrier((image_part, far_images))
    far_weights = weigh(far_images, far_place, texts, c)
    weights = jnp.concatenate([weights, far_weights], axis=0)
    images = jnp.concatenate([images, far_images], axis=0)
    part = product(weights.T, images).astype(bf16).reshape(NX, half_rows, d)
    ways = (0, 1 + 2 * c, 2, 3 - 2 * c)
    blocks = [rows_at(part, (x + k) & (NX - 1), 1).reshape(half_rows, d) for k in ways]
    image_parts = exchange(image_part.reshape(NZ, R, d), "z", 3)
    unit_grad_image = image_parts.astype(f32).sum(axis=0)

    received = [shift(blocks[2], "x", NX, 2), cross(blocks[1], 1), cross(blocks[3], 3)]
    image_grad = tangent(unit_grad_image, image_unit, image_gain)
    total, image_grad = lax.optimization_barrier((blocks[0], image_grad))
    total = total.astype(f32) + sum(block.astype(f32) for block in received)
    total = total.astype(bf16).reshape(NY, R, d)
    unit_grad_text = exchange(total, "y", FIRST_Y).astype(f32).sum(axis=0)

    return image_grad, tangent(unit_grad_text, text_unit, text_gain)


def solution(mesh):
    fine = Mesh(mesh.devices.reshape(NY, NZ, NX, NC), AXES)
    image = ("y", "z", "x", "core")
    text = ("z", "x", "core", "y")
    return jax.shard_map(
        shards,
        mesh=fine,
        in_specs=(P(image, None), P(image), P(text, None), P(text), P("y"), P(), P()),
        out_specs=(P(image, None), P(text, None)),
        check_vma=False,
    )
```

```python
import jax
import jax.numpy as jnp
from jax import lax
from jax.experimental import pallas as pl
from jax.experimental.pallas import tpu as pltpu
from jax.sharding import Mesh, PartitionSpec as P

epsilon = 1e-06
AXES = ("y", "z", "x", "core")
NY, NZ, NX, NC = 8, 12, 4, 2
FIRST_Y, FIRST_Z = 4, 10
R = 8
f32 = jnp.float32
bf16 = jnp.bfloat16


def unit_rows(mantissa_ref, exponent_ref):
    row = lax.broadcasted_iota(jnp.int32, (R, 1), 0)
    exponent = jnp.zeros((R, 1), jnp.int32)
    for r in range(R):
        exponent = jnp.where(row == r, exponent_ref[r], exponent)
    scaled = mantissa_ref[...].astype(f32) * jnp.exp2(exponent.astype(f32))
    norm = jnp.sqrt(jnp.sum(scaled * scaled, axis=1, keepdims=True) + epsilon)
    return norm, scaled / norm


def text_kernel(mantissa_ref, exponent_ref, send_ref):
    _, unit = unit_rows(mantissa_ref, exponent_ref)
    half = unit.astype(bf16)
    for k in range(NY):
        send_ref[k] = half


def image_kernel(
    image_ref, image_exponent_ref, text_ref, text_exponent_ref, scale_ref, bias_ref,
    send_ref, image_unit_ref, image_gain_ref, text_unit_ref, text_gain_ref, scale_row_ref, bias_row_ref,
):
    norm, unit = unit_rows(image_ref, image_exponent_ref)
    half = unit.astype(bf16)
    for k in range(NZ):
        send_ref[k] = half
    factor = scale_ref[0]
    image_unit_ref[...] = unit
    image_gain_ref[...] = jnp.broadcast_to(factor / norm, unit.shape)
    norm, unit = unit_rows(text_ref, text_exponent_ref)
    text_unit_ref[...] = unit
    text_gain_ref[...] = jnp.broadcast_to(factor / norm, unit.shape)
    scale_row_ref[...] = jnp.full(scale_row_ref.shape, factor, f32)
    bias_row_ref[...] = jnp.full(bias_row_ref.shape, bias_ref[0], f32)


vmem = pl.BlockSpec(memory_space=pltpu.VMEM)
smem = pl.BlockSpec(memory_space=pltpu.SMEM)


def text_prologue(mantissa, exponent):
    return pl.pallas_call(
        text_kernel,
        out_shape=jax.ShapeDtypeStruct((NY,) + mantissa.shape, bf16),
        in_specs=[vmem, smem],
        out_specs=vmem,
    )(mantissa, exponent)


def image_prologue(image, image_exponent, text, text_exponent, scale, bias):
    d = image.shape[1]
    rows = jax.ShapeDtypeStruct((R, d), f32)
    row = jax.ShapeDtypeStruct((1, NX * NY * R), f32)
    return pl.pallas_call(
        image_kernel,
        out_shape=(
            jax.ShapeDtypeStruct((NZ, R, d), bf16), rows, rows, rows, rows, row, row,
        ),
        in_specs=[vmem, smem, vmem, smem, smem, smem],
        out_specs=(vmem,) * 7,
    )(image, image_exponent, text, text_exponent, scale, bias)


def exchange(blocks, axis, first=0):
    n = blocks.shape[0]
    order = [[(first + k) % n for k in range(n)]]
    return lax.all_to_all(blocks, axis, split_axis=0, concat_axis=0, axis_index_groups=order, tiled=True)


def shift(block, axis, n, k):
    return lax.ppermute(block, axis, [(i, (i + k) % n) for i in range(n)])


def cross(block, k):
    moves = [(x * NC + c, (x + (k if c == 0 else -k)) % NX * NC + c) for x in range(NX) for c in range(NC)]
    return lax.ppermute(block, ("x", "core"), moves)


def rows_at(array, start, size):
    starts = (start,) + (jnp.int32(0),) * (array.ndim - 1)
    return lax.dynamic_slice(array, starts, (size,) + array.shape[1:], allow_negative_indices=False)


def product(a, b):
    return jnp.dot(a, b, preferred_element_type=f32)


def tangent(unit_grad, unit, gain):
    return (unit_grad - unit * jnp.sum(unit * unit_grad, axis=1, keepdims=True)) * gain


def shards(
    image_mantissa, image_exponent, text_mantissa, text_exponent, positive, logit_scale, logit_bias
):
    d = image_mantissa.shape[1]
    z, x, c = lax.axis_index("z"), lax.axis_index("x"), lax.axis_index("core")
    half_rows = NY * R
    near_rows = NX * half_rows
    own = NZ * R

    place = positive.reshape(NZ, NX * NC, R).transpose(1, 0, 2).reshape(NX * NC, own)
    place = place - z * (NX * NC * half_rows)
    far_place = jnp.roll(rows_at(place, x * NC + 1 - c, 1).reshape(own), -FIRST_Z * R)
    place = jnp.roll(rows_at(place, x * NC + c, 1).reshape(own), -FIRST_Z * R)

    text_send = text_prologue(text_mantissa, text_exponent)
    image_mantissa, place, far_place = lax.optimization_barrier((image_mantissa, place, far_place))
    image_send, image_unit, image_gain, text_unit, text_gain, scale, bias = image_prologue(
        image_mantissa, image_exponent, text_mantissa, text_exponent, logit_scale, logit_bias
    )
    texts = lax.all_gather(exchange(text_send, "y", FIRST_Y).reshape(half_rows, d), "x", axis=0, tiled=True)
    far_texts = shift(texts, "core", NC, 1)
    images = exchange(image_send, "z", FIRST_Z).reshape(own, d)
    far_images = shift(images, "core", NC, 1)

    column = jnp.arange(near_rows, dtype=jnp.int32)[None, :]

    def weigh(images, place, texts, core):
        target = (column // half_rows * NC + core) * half_rows + (column + FIRST_Y * R) % half_rows
        logits = scale * product(images, texts.T) + bias
        label_sign = jnp.where(place[:, None] == target, 1.0, -1.0).astype(f32)
        return (-label_sign * jax.nn.sigmoid(-label_sign * logits)).astype(bf16)

    weights = weigh(images, place, texts, c)
    near = lax.optimization_barrier(product(jnp.roll(weights, (FIRST_Z - 3) * R, axis=0), texts))
    cross_weights = jnp.roll(weigh(images, place, far_texts, 1 - c), (FIRST_Z - 3) * R, axis=0)
    image_part = (near + product(cross_weights, far_texts)).astype(bf16)

    image_part, far_images = lax.optimization_barrier((image_part, far_images))
    far_weights = weigh(far_images, far_place, texts, c)
    weights = jnp.concatenate([weights, far_weights], axis=0)
    images = jnp.concatenate([images, far_images], axis=0)
    part = product(weights.T, images).astype(bf16).reshape(NX, half_rows, d)
    ways = range(NX)
    blocks = [rows_at(part, (x + k) & (NX - 1), 1).reshape(half_rows, d) for k in ways]
    image_parts = exchange(image_part.reshape(NZ, R, d), "z", 3)
    unit_grad_image = image_parts.astype(f32).sum(axis=0)

    opposite = shift(blocks[2], "x", NX, 2)
    received = [opposite, shift(blocks[1], "x", NX, 1), shift(blocks[3], "x", NX, 3)]
    image_grad = tangent(unit_grad_image, image_unit, image_gain)
    total, image_grad = lax.optimization_barrier((blocks[0], image_grad))
    total = total.astype(f32) + sum(block.astype(f32) for block in received)
    total = total.astype(bf16).reshape(NY, R, d)
    unit_grad_text = exchange(total, "y", FIRST_Y).astype(f32).sum(axis=0)

    return image_grad, tangent(unit_grad_text, text_unit, text_gain)


def solution(mesh):
    fine = Mesh(mesh.devices.reshape(NY, NZ, NX, NC), AXES)
    image = ("y", "z", "x", "core")
    text = ("z", "x", "core", "y")
    return jax.shard_map(
        shards,
        mesh=fine,
        in_specs=(P(image, None), P(image), P(text, None), P(text), P("y"), P(), P()),
        out_specs=(P(image, None), P(text, None)),
        check_vma=False,
    )
```

```python
import jax
import jax.numpy as jnp
from jax import lax
from jax.experimental import pallas as pl
from jax.experimental.pallas import tpu as pltpu
from jax.sharding import Mesh, PartitionSpec as P

epsilon = 1e-06
AXES = ("y", "z", "x", "core")
NY, NZ, NX, NC = 8, 12, 4, 2
FIRST_Z = 10
Y_ORDER = [4, 0, 1, 7, 2, 6, 3, 5]
R = 8
f32 = jnp.float32
bf16 = jnp.bfloat16


def unit_rows(mantissa_ref, exponent_ref):
    row = lax.broadcasted_iota(jnp.int32, (R, 1), 0)
    exponent = jnp.zeros((R, 1), jnp.int32)
    for r in range(R):
        exponent = jnp.where(row == r, exponent_ref[r], exponent)
    scaled = mantissa_ref[...].astype(f32) * jnp.exp2(exponent.astype(f32))
    norm = jnp.sqrt(jnp.sum(scaled * scaled, axis=1, keepdims=True) + epsilon)
    return norm, scaled / norm


def text_kernel(mantissa_ref, exponent_ref, send_ref):
    _, unit = unit_rows(mantissa_ref, exponent_ref)
    half = unit.astype(bf16)
    for k in range(NY):
        send_ref[k] = half


def image_kernel(
    image_ref, image_exponent_ref, text_ref, text_exponent_ref, scale_ref, bias_ref,
    send_ref, image_unit_ref, image_gain_ref, text_unit_ref, text_gain_ref, scale_row_ref, bias_row_ref,
):
    norm, unit = unit_rows(image_ref, image_exponent_ref)
    half = unit.astype(bf16)
    for k in range(NZ):
        send_ref[k] = half
    factor = scale_ref[0]
    image_unit_ref[...] = unit
    image_gain_ref[...] = jnp.broadcast_to(factor / norm, unit.shape)
    norm, unit = unit_rows(text_ref, text_exponent_ref)
    text_unit_ref[...] = unit
    text_gain_ref[...] = jnp.broadcast_to(factor / norm, unit.shape)
    scale_row_ref[...] = jnp.full(scale_row_ref.shape, factor, f32)
    bias_row_ref[...] = jnp.full(bias_row_ref.shape, bias_ref[0], f32)


vmem = pl.BlockSpec(memory_space=pltpu.VMEM)
smem = pl.BlockSpec(memory_space=pltpu.SMEM)


def text_prologue(mantissa, exponent):
    return pl.pallas_call(
        text_kernel,
        out_shape=jax.ShapeDtypeStruct((NY,) + mantissa.shape, bf16),
        in_specs=[vmem, smem],
        out_specs=vmem,
    )(mantissa, exponent)


def image_prologue(image, image_exponent, text, text_exponent, scale, bias):
    d = image.shape[1]
    rows = jax.ShapeDtypeStruct((R, d), f32)
    row = jax.ShapeDtypeStruct((1, NX * NY * R), f32)
    return pl.pallas_call(
        image_kernel,
        out_shape=(
            jax.ShapeDtypeStruct((NZ, R, d), bf16), rows, rows, rows, rows, row, row,
        ),
        in_specs=[vmem, smem, vmem, smem, smem, smem],
        out_specs=(vmem,) * 7,
    )(image, image_exponent, text, text_exponent, scale, bias)


def ring(n, first):
    return [(first + k) % n for k in range(n)]


def exchange(blocks, axis, order):
    return lax.all_to_all(blocks, axis, split_axis=0, concat_axis=0, axis_index_groups=[order], tiled=True)


def shift(block, axis, n, k):
    return lax.ppermute(block, axis, [(i, (i + k) % n) for i in range(n)])


def rows_at(array, start, size):
    starts = (start,) + (jnp.int32(0),) * (array.ndim - 1)
    return lax.dynamic_slice(array, starts, (size,) + array.shape[1:], allow_negative_indices=False)


def product(a, b):
    return jnp.dot(a, b, preferred_element_type=f32)


def tangent(unit_grad, unit, gain):
    return (unit_grad - unit * jnp.sum(unit * unit_grad, axis=1, keepdims=True)) * gain


def shards(
    image_mantissa, image_exponent, text_mantissa, text_exponent, positive, logit_scale, logit_bias
):
    d = image_mantissa.shape[1]
    z, x, c = lax.axis_index("z"), lax.axis_index("x"), lax.axis_index("core")
    half_rows = NY * R
    near_rows = NX * half_rows
    own = NZ * R

    place = positive.reshape(NZ, NX * NC, R).transpose(1, 0, 2).reshape(NX * NC, own)
    place = place - z * (NX * NC * half_rows)
    far_place = jnp.roll(rows_at(place, x * NC + 1 - c, 1).reshape(own), -FIRST_Z * R)
    place = jnp.roll(rows_at(place, x * NC + c, 1).reshape(own), -FIRST_Z * R)

    text_send = text_prologue(text_mantissa, text_exponent)
    image_mantissa, place, far_place = lax.optimization_barrier((image_mantissa, place, far_place))
    image_send, image_unit, image_gain, text_unit, text_gain, scale, bias = image_prologue(
        image_mantissa, image_exponent, text_mantissa, text_exponent, logit_scale, logit_bias
    )
    texts = lax.all_gather(exchange(text_send, "y", Y_ORDER).reshape(half_rows, d), "x", axis=0, tiled=True)
    far_texts = shift(texts, "core", NC, 1)
    images = exchange(image_send, "z", ring(NZ, FIRST_Z)).reshape(own, d)
    far_images = shift(images, "core", NC, 1)

    column = jnp.arange(near_rows, dtype=jnp.int32)[None, :]
    held = jnp.asarray([k * R + r for _ in range(NX) for k in Y_ORDER for r in range(R)], jnp.int32)[None, :]

    def weigh(images, place, texts, core):
        target = (column // half_rows * NC + core) * half_rows + held
        logits = scale * product(images, texts.T) + bias
        label_sign = jnp.where(place[:, None] == target, 1.0, -1.0).astype(f32)
        return (-label_sign * jax.nn.sigmoid(-label_sign * logits)).astype(bf16)

    weights = weigh(images, place, texts, c)
    near = lax.optimization_barrier(product(jnp.roll(weights, (FIRST_Z - 3) * R, axis=0), texts))
    cross_weights = jnp.roll(weigh(images, place, far_texts, 1 - c), (FIRST_Z - 3) * R, axis=0)
    image_part = (near + product(cross_weights, far_texts)).astype(bf16)

    image_part, far_images = lax.optimization_barrier((image_part, far_images))
    far_weights = weigh(far_images, far_place, texts, c)
    weights = jnp.concatenate([weights, far_weights], axis=0)
    images = jnp.concatenate([images, far_images], axis=0)
    part = product(weights.T, images).astype(bf16).reshape(NX, half_rows, d)
    ways = range(NX)
    blocks = [rows_at(part, (x + k) & (NX - 1), 1).reshape(half_rows, d) for k in ways]
    image_parts = exchange(image_part.reshape(NZ, R, d), "z", ring(NZ, 3))
    unit_grad_image = image_parts.astype(f32).sum(axis=0)

    opposite = shift(blocks[2], "x", NX, 2)
    received = [opposite, shift(blocks[1], "x", NX, 1), shift(blocks[3], "x", NX, 3)]
    image_grad = tangent(unit_grad_image, image_unit, image_gain)
    total, image_grad = lax.optimization_barrier((blocks[0], image_grad))
    total = total.astype(f32) + sum(block.astype(f32) for block in received)
    total = total.astype(bf16).reshape(NY, R, d)
    unit_grad_text = exchange(total, "y", Y_ORDER).astype(f32).sum(axis=0)

    return image_grad, tangent(unit_grad_text, text_unit, text_gain)


def solution(mesh):
    fine = Mesh(mesh.devices.reshape(NY, NZ, NX, NC), AXES)
    image = ("y", "z", "x", "core")
    text = ("z", "x", "core", "y")
    return jax.shard_map(
        shards,
        mesh=fine,
        in_specs=(P(image, None), P(image), P(text, None), P(text), P("y"), P(), P()),
        out_specs=(P(image, None), P(text, None)),
        check_vma=False,
    )
```

```python
import jax
import jax.numpy as jnp
from jax import lax
from jax.experimental import pallas as pl
from jax.experimental.pallas import tpu as pltpu
from jax.sharding import Mesh, PartitionSpec as P

epsilon = 1e-06
AXES = ("y", "z", "x", "core")
NY, NZ, NX, NC = 8, 12, 4, 2
Z_RETURN = [3, 9, 8, 10, 7, 11, 0, 6, 1, 5, 2, 4]
TURN = Z_RETURN.index(10)
Z_ORDER = Z_RETURN[TURN:] + Z_RETURN[:TURN]
Y_ORDER = [4, 0, 1, 7, 2, 6, 3, 5]
R = 8
f32 = jnp.float32
bf16 = jnp.bfloat16


def unit_rows(mantissa_ref, exponent_ref):
    row = lax.broadcasted_iota(jnp.int32, (R, 1), 0)
    exponent = jnp.zeros((R, 1), jnp.int32)
    for r in range(R):
        exponent = jnp.where(row == r, exponent_ref[r], exponent)
    scaled = mantissa_ref[...].astype(f32) * jnp.exp2(exponent.astype(f32))
    norm = jnp.sqrt(jnp.sum(scaled * scaled, axis=1, keepdims=True) + epsilon)
    return norm, scaled / norm


def text_kernel(mantissa_ref, exponent_ref, send_ref):
    _, unit = unit_rows(mantissa_ref, exponent_ref)
    half = unit.astype(bf16)
    for k in range(NY):
        send_ref[k] = half


def image_kernel(
    image_ref, image_exponent_ref, text_ref, text_exponent_ref, scale_ref, bias_ref,
    send_ref, image_unit_ref, image_gain_ref, text_unit_ref, text_gain_ref, scale_row_ref, bias_row_ref,
):
    norm, unit = unit_rows(image_ref, image_exponent_ref)
    half = unit.astype(bf16)
    for k in range(NZ):
        send_ref[k] = half
    factor = scale_ref[0]
    image_unit_ref[...] = unit
    image_gain_ref[...] = jnp.broadcast_to(factor / norm, unit.shape)
    norm, unit = unit_rows(text_ref, text_exponent_ref)
    text_unit_ref[...] = unit
    text_gain_ref[...] = jnp.broadcast_to(factor / norm, unit.shape)
    scale_row_ref[...] = jnp.full(scale_row_ref.shape, factor, f32)
    bias_row_ref[...] = jnp.full(bias_row_ref.shape, bias_ref[0], f32)


vmem = pl.BlockSpec(memory_space=pltpu.VMEM)
smem = pl.BlockSpec(memory_space=pltpu.SMEM)


def text_prologue(mantissa, exponent):
    return pl.pallas_call(
        text_kernel,
        out_shape=jax.ShapeDtypeStruct((NY,) + mantissa.shape, bf16),
        in_specs=[vmem, smem],
        out_specs=vmem,
    )(mantissa, exponent)


def image_prologue(image, image_exponent, text, text_exponent, scale, bias):
    d = image.shape[1]
    rows = jax.ShapeDtypeStruct((R, d), f32)
    row = jax.ShapeDtypeStruct((1, NX * NY * R), f32)
    return pl.pallas_call(
        image_kernel,
        out_shape=(
            jax.ShapeDtypeStruct((NZ, R, d), bf16), rows, rows, rows, rows, row, row,
        ),
        in_specs=[vmem, smem, vmem, smem, smem, smem],
        out_specs=(vmem,) * 7,
    )(image, image_exponent, text, text_exponent, scale, bias)


def by_order(place):
    return jnp.concatenate([place[k * R : (k + 1) * R] for k in Z_ORDER])


def exchange(blocks, axis, order):
    return lax.all_to_all(blocks, axis, split_axis=0, concat_axis=0, axis_index_groups=[order], tiled=True)


def shift(block, axis, n, k):
    return lax.ppermute(block, axis, [(i, (i + k) % n) for i in range(n)])


def rows_at(array, start, size):
    starts = (start,) + (jnp.int32(0),) * (array.ndim - 1)
    return lax.dynamic_slice(array, starts, (size,) + array.shape[1:], allow_negative_indices=False)


def product(a, b):
    return jnp.dot(a, b, preferred_element_type=f32)


def tangent(unit_grad, unit, gain):
    return (unit_grad - unit * jnp.sum(unit * unit_grad, axis=1, keepdims=True)) * gain


def shards(
    image_mantissa, image_exponent, text_mantissa, text_exponent, positive, logit_scale, logit_bias
):
    d = image_mantissa.shape[1]
    z, x, c = lax.axis_index("z"), lax.axis_index("x"), lax.axis_index("core")
    half_rows = NY * R
    near_rows = NX * half_rows
    own = NZ * R

    place = positive.reshape(NZ, NX * NC, R).transpose(1, 0, 2).reshape(NX * NC, own)
    place = place - z * (NX * NC * half_rows)
    far_place = by_order(rows_at(place, x * NC + 1 - c, 1).reshape(own))
    place = by_order(rows_at(place, x * NC + c, 1).reshape(own))

    text_send = text_prologue(text_mantissa, text_exponent)
    image_mantissa, place, far_place = lax.optimization_barrier((image_mantissa, place, far_place))
    image_send, image_unit, image_gain, text_unit, text_gain, scale, bias = image_prologue(
        image_mantissa, image_exponent, text_mantissa, text_exponent, logit_scale, logit_bias
    )
    texts = lax.all_gather(exchange(text_send, "y", Y_ORDER).reshape(half_rows, d), "x", axis=0, tiled=True)
    far_texts = shift(texts, "core", NC, 1)
    images = exchange(image_send, "z", Z_ORDER).reshape(own, d)
    far_images = shift(images, "core", NC, 1)

    column = jnp.arange(near_rows, dtype=jnp.int32)[None, :]
    held = jnp.asarray([k * R + r for _ in range(NX) for k in Y_ORDER for r in range(R)], jnp.int32)[None, :]

    def weigh(images, place, texts, core):
        target = (column // half_rows * NC + core) * half_rows + held
        logits = scale * product(images, texts.T) + bias
        label_sign = jnp.where(place[:, None] == target, 1.0, -1.0).astype(f32)
        return (-label_sign * jax.nn.sigmoid(-label_sign * logits)).astype(bf16)

    weights = weigh(images, place, texts, c)
    near = lax.optimization_barrier(product(jnp.roll(weights, TURN * R, axis=0), texts))
    cross_weights = jnp.roll(weigh(images, place, far_texts, 1 - c), TURN * R, axis=0)
    image_part = (near + product(cross_weights, far_texts)).astype(bf16)

    image_part, far_images = lax.optimization_barrier((image_part, far_images))
    far_weights = weigh(far_images, far_place, texts, c)
    weights = jnp.concatenate([weights, far_weights], axis=0)
    images = jnp.concatenate([images, far_images], axis=0)
    part = product(weights.T, images).astype(bf16).reshape(NX, half_rows, d)
    ways = range(NX)
    blocks = [rows_at(part, (x + k) & (NX - 1), 1).reshape(half_rows, d) for k in ways]
    image_parts = exchange(image_part.reshape(NZ, R, d), "z", Z_RETURN)
    unit_grad_image = image_parts.astype(f32).sum(axis=0)

    opposite = shift(blocks[2], "x", NX, 2)
    received = [opposite, shift(blocks[1], "x", NX, 1), shift(blocks[3], "x", NX, 3)]
    image_grad = tangent(unit_grad_image, image_unit, image_gain)
    total, image_grad = lax.optimization_barrier((blocks[0], image_grad))
    total = total.astype(f32) + sum(block.astype(f32) for block in received)
    total = total.astype(bf16).reshape(NY, R, d)
    unit_grad_text = exchange(total, "y", Y_ORDER).astype(f32).sum(axis=0)

    return image_grad, tangent(unit_grad_text, text_unit, text_gain)


def solution(mesh):
    fine = Mesh(mesh.devices.reshape(NY, NZ, NX, NC), AXES)
    image = ("y", "z", "x", "core")
    text = ("z", "x", "core", "y")
    return jax.shard_map(
        shards,
        mesh=fine,
        in_specs=(P(image, None), P(image), P(text, None), P(text), P("y"), P(), P()),
        out_specs=(P(image, None), P(text, None)),
        check_vma=False,
    )
```

```python
import jax
import jax.numpy as jnp
from jax import lax
from jax.experimental import pallas as pl
from jax.experimental.pallas import tpu as pltpu
from jax.sharding import Mesh, PartitionSpec as P

epsilon = 1e-06
AXES = ("y", "z", "x", "core")
NY, NZ, NX, NC = 8, 12, 4, 2
FIRST_Z, FIRST_X = 10, 2
Y_ORDER = [4, 0, 1, 7, 2, 6, 3, 5]
R = 8
f32 = jnp.float32
bf16 = jnp.bfloat16


def unit_rows(mantissa_ref, exponent_ref):
    row = lax.broadcasted_iota(jnp.int32, (R, 1), 0)
    exponent = jnp.zeros((R, 1), jnp.int32)
    for r in range(R):
        exponent = jnp.where(row == r, exponent_ref[r], exponent)
    scaled = mantissa_ref[...].astype(f32) * jnp.exp2(exponent.astype(f32))
    norm = jnp.sqrt(jnp.sum(scaled * scaled, axis=1, keepdims=True) + epsilon)
    return norm, scaled / norm


def text_kernel(mantissa_ref, exponent_ref, send_ref):
    _, unit = unit_rows(mantissa_ref, exponent_ref)
    half = unit.astype(bf16)
    for k in range(NY):
        send_ref[k] = half


def image_kernel(
    image_ref, image_exponent_ref, text_ref, text_exponent_ref, affine_ref,
    send_ref, image_unit_ref, image_gain_ref, text_unit_ref, text_gain_ref, scale_row_ref, bias_row_ref,
):
    norm, unit = unit_rows(image_ref, image_exponent_ref)
    half = unit.astype(bf16)
    for k in range(NZ):
        send_ref[k] = half
    factor = affine_ref[0]
    image_unit_ref[...] = unit
    image_gain_ref[...] = jnp.broadcast_to(factor / norm, unit.shape)
    norm, unit = unit_rows(text_ref, text_exponent_ref)
    text_unit_ref[...] = unit
    text_gain_ref[...] = jnp.broadcast_to(factor / norm, unit.shape)
    scale_row_ref[...] = jnp.full(scale_row_ref.shape, factor, f32)
    bias_row_ref[...] = jnp.full(bias_row_ref.shape, affine_ref[1], f32)


vmem = pl.BlockSpec(memory_space=pltpu.VMEM)
smem = pl.BlockSpec(memory_space=pltpu.SMEM)


def text_prologue(mantissa, exponent):
    return pl.pallas_call(
        text_kernel,
        out_shape=jax.ShapeDtypeStruct((NY,) + mantissa.shape, bf16),
        in_specs=[vmem, smem],
        out_specs=vmem,
    )(mantissa, exponent)


def image_prologue(image, image_exponent, text, text_exponent, affine):
    d = image.shape[1]
    rows = jax.ShapeDtypeStruct((R, d), f32)
    row = jax.ShapeDtypeStruct((1, NX * NY * R), f32)
    return pl.pallas_call(
        image_kernel,
        out_shape=(
            jax.ShapeDtypeStruct((NZ, R, d), bf16), rows, rows, rows, rows, row, row,
        ),
        in_specs=[vmem, smem, vmem, smem, smem],
        out_specs=(vmem,) * 7,
    )(image, image_exponent, text, text_exponent, affine)


def ring(n, first):
    return [(first + k) % n for k in range(n)]


def exchange(blocks, axis, order):
    return lax.all_to_all(blocks, axis, split_axis=0, concat_axis=0, axis_index_groups=[order], tiled=True)


def shift(block, axis, n, k):
    return lax.ppermute(block, axis, [(i, (i + k) % n) for i in range(n)])


def rows_at(array, start, size):
    starts = (start,) + (jnp.int32(0),) * (array.ndim - 1)
    return lax.dynamic_slice(array, starts, (size,) + array.shape[1:], allow_negative_indices=False)


def product(a, b):
    return jnp.dot(a, b, preferred_element_type=f32)


def tangent(unit_grad, unit, gain):
    return (unit_grad - unit * jnp.sum(unit * unit_grad, axis=1, keepdims=True)) * gain


def shards(
    image_mantissa, image_exponent, text_mantissa, text_exponent, positive, logit_scale, logit_bias
):
    d = image_mantissa.shape[1]
    z, x, c = lax.axis_index("z"), lax.axis_index("x"), lax.axis_index("core")
    half_rows = NY * R
    near_rows = NX * half_rows
    own = NZ * R

    place = positive.reshape(NZ, NX * NC, R).transpose(1, 0, 2).reshape(NX * NC, own)
    place = place - z * (NX * NC * half_rows)
    far_place = jnp.roll(rows_at(place, x * NC + 1 - c, 1).reshape(own), -FIRST_Z * R)
    place = jnp.roll(rows_at(place, x * NC + c, 1).reshape(own), -FIRST_Z * R)

    text_send = text_prologue(text_mantissa, text_exponent)
    image_mantissa, place, far_place = lax.optimization_barrier((image_mantissa, place, far_place))
    image_send, image_unit, image_gain, text_unit, text_gain, scale, bias = image_prologue(
        image_mantissa, image_exponent, text_mantissa, text_exponent, jnp.concatenate([logit_scale, logit_bias])
    )
    texts = lax.all_gather(exchange(text_send, "y", Y_ORDER).reshape(half_rows, d), "x", axis=0, tiled=True, axis_index_groups=[ring(NX, FIRST_X)])
    far_texts = shift(texts, "core", NC, 1)
    images = exchange(image_send, "z", ring(NZ, FIRST_Z)).reshape(own, d)
    far_images = shift(images, "core", NC, 1)

    column = jnp.arange(near_rows, dtype=jnp.int32)[None, :]
    held = jnp.asarray([k * R + r for _ in range(NX) for k in Y_ORDER for r in range(R)], jnp.int32)[None, :]

    def weigh(images, place, texts, core):
        target = ((column // half_rows + FIRST_X) % NX * NC + core) * half_rows + held
        logits = scale * product(images, texts.T) + bias
        label_sign = jnp.where(place[:, None] == target, 1.0, -1.0).astype(f32)
        return (-label_sign * jax.nn.sigmoid(-label_sign * logits)).astype(bf16)

    weights = weigh(images, place, texts, c)
    near = lax.optimization_barrier(product(jnp.roll(weights, (FIRST_Z - 3) * R, axis=0), texts))
    cross_weights = jnp.roll(weigh(images, place, far_texts, 1 - c), (FIRST_Z - 3) * R, axis=0)
    image_part = (near + product(cross_weights, far_texts)).astype(bf16)

    image_part, far_images = lax.optimization_barrier((image_part, far_images))
    far_weights = weigh(far_images, far_place, texts, c)
    weights = jnp.concatenate([weights, far_weights], axis=0)
    images = jnp.concatenate([images, far_images], axis=0)
    part = product(weights.T, images).astype(bf16).reshape(NX, half_rows, d)
    ways = range(NX)
    blocks = [rows_at(part, (x + k - FIRST_X) & (NX - 1), 1).reshape(half_rows, d) for k in ways]
    image_parts = exchange(image_part.reshape(NZ, R, d), "z", ring(NZ, 3))
    unit_grad_image = image_parts.astype(f32).sum(axis=0)

    opposite = shift(blocks[2], "x", NX, 2)
    received = [opposite, shift(blocks[1], "x", NX, 1), shift(blocks[3], "x", NX, 3)]
    image_grad = tangent(unit_grad_image, image_unit, image_gain)
    total, image_grad = lax.optimization_barrier((blocks[0], image_grad))
    total = total.astype(f32) + sum(block.astype(f32) for block in received)
    total = total.astype(bf16).reshape(NY, R, d)
    unit_grad_text = exchange(total, "y", Y_ORDER).astype(f32).sum(axis=0)

    return image_grad, tangent(unit_grad_text, text_unit, text_gain)


def solution(mesh):
    fine = Mesh(mesh.devices.reshape(NY, NZ, NX, NC), AXES)
    image = ("y", "z", "x", "core")
    text = ("z", "x", "core", "y")
    return jax.shard_map(
        shards,
        mesh=fine,
        in_specs=(P(image, None), P(image), P(text, None), P(text), P("y"), P(), P()),
        out_specs=(P(image, None), P(text, None)),
        check_vma=False,
    )
```
